256 devices in a mesh: img: 32 (over z, x), txt: 8 (over y, core).
Axes of the slice: x: 4, y: 4, z: 8, core: 2. Of those that a mesh axis runs over, the one named last changes fastest.
Arguments:
- image_pooled: bfloat16 [16384, 1664], P('img', 'txt'), may hold values from -6 to 6
- text_pooled: bfloat16 [16384, 1280], P('txt', 'img'), may hold values from -6 to 6
- image_proj: bfloat16 [1664, 1280], P('txt'), may hold values from -1.5 to 1.5
- text_proj: bfloat16 [1280, 1280], P('img'), may hold values from -2 to 2
- teacher_scale: float32 [1], replicated, may hold values from 280 to 400
Outputs:
- image_targets: float32 [16384, 16384], P('img', 'txt')
- text_targets: float32 [16384, 16384], P('img', 'txt')
The draws below stay inside these ranges and needn't reach their ends.
All inputs are finite; a program needn't handle non-finite values.
Results may differ from the reference program's by a relative error of at most 0.0011.
Values may be sent and summed in bfloat16 or wider, within the bound.
No kernel may reach another device: no remote copies, remote signals or barrier semaphores. Data moves between devices by JAX's collectives and lax.ppermute only.
A program may use at most 64 MiB of HBM per device.

```python
import math
import jax
import jax.numpy as jnp
from jax import lax

D_IMG = 1664
D_TXT = 1280
EMBED = 1280
BATCH = 16384


lead_levels = ((6.0, 5.0, 2.5), (6.0, 4.0, -6.0), (6.0, 3.0, 2.0), (6.0,))


def lead_plan(key):
    plan_key = jax.random.fold_in(key, 100)
    image_lines = jax.random.permutation(jax.random.fold_in(plan_key, 1), D_IMG)[:4]
    text_lines = jax.random.permutation(jax.random.fold_in(plan_key, 2), D_TXT)[:4]
    directions = jax.random.uniform(jax.random.fold_in(plan_key, 3), (5, EMBED), jnp.float32, -1.0, 1.0)
    directions = directions.at[:, 0].set(1.0).at[:, 1].set(-1.0)
    return (image_lines, text_lines, directions)


def grouped_rows(centers, noise_draw, lead_columns, key):
    place_key, rest_key = jax.random.split(key)
    grouped = jnp.repeat(centers, 16, axis=0) + 0.15 * noise_draw
    chosen = jax.random.permutation(place_key, grouped.shape[0])[:10]
    lead_value = jax.random.uniform(rest_key, (grouped.shape[0], 4), jnp.float32, -0.2, 0.2)
    counter = 0
    for position, strengths in enumerate(lead_levels):
        for strength in strengths:
            lead_value = lead_value.at[chosen[counter], position].set(strength)
            counter = counter + 1
    grouped = grouped.at[:, lead_columns].set(lead_value)
    return jnp.clip(grouped, -6.0, 6.0)


def draw_image_pooled(key, part):
    image_lines, text_lines, directions = lead_plan(key)
    key = jax.random.fold_in(key, 1)
    center_key, noise_key, lead_key = jax.random.split(key, 3)
    centers = jnp.clip(jax.random.normal(center_key, (BATCH // 16, D_IMG), jnp.float32), -6.0, 6.0)
    noise_draw = jnp.clip(jax.random.normal(noise_key, (BATCH, D_IMG), jnp.float32), -6.0, 6.0)
    return grouped_rows(centers, noise_draw, image_lines, lead_key).astype(jnp.bfloat16)


def draw_text_pooled(key, part):
    image_lines, text_lines, directions = lead_plan(key)
    key = jax.random.fold_in(key, 2)
    center_key, noise_key, lead_key = jax.random.split(key, 3)
    centers = jnp.clip(jax.random.normal(center_key, (BATCH // 16, D_TXT), jnp.float32), -6.0, 6.0)
    noise_draw = jnp.clip(jax.random.normal(noise_key, (BATCH, D_TXT), jnp.float32), -6.0, 6.0)
    return grouped_rows(centers, noise_draw, text_lines, lead_key).astype(jnp.bfloat16)


def draw_image_proj(key, part):
    image_lines, text_lines, directions = lead_plan(key)
    key = jax.random.fold_in(key, 3)
    weight_draw = jnp.clip(jax.random.normal(key, (D_IMG, EMBED), jnp.float32), -6.0, 6.0) / math.sqrt(D_IMG)
    return weight_draw.at[image_lines].set(1.5 * directions[:4]).astype(jnp.bfloat16)


def draw_text_proj(key, part):
    image_lines, text_lines, directions = lead_plan(key)
    key = jax.random.fold_in(key, 4)
    weight_draw = jnp.clip(jax.random.normal(key, (D_TXT, EMBED), jnp.float32), -6.0, 6.0) / math.sqrt(D_TXT)
    planted = jnp.concatenate([directions[:3], directions[4:]], axis=0)
    return weight_draw.at[text_lines].set(2.0 * planted).astype(jnp.bfloat16)


def setup_inputs(seed: int = 0) -> dict:
    keys = jax.random.split(jax.random.key(seed), 6)
    return {
        "image_pooled": draw_image_pooled(jax.random.fold_in(keys[5], 71), 0),
        "text_pooled": draw_text_pooled(jax.random.fold_in(keys[5], 71), 0),
        "image_proj": draw_image_proj(jax.random.fold_in(keys[5], 71), 0),
        "text_proj": draw_text_proj(jax.random.fold_in(keys[5], 71), 0),
        "teacher_scale": jnp.clip(jnp.exp(jax.random.uniform(keys[4], (1,), jnp.float32, math.log(280.0), math.log(400.0))), 280.0, 400.0),
    }


def unit_rows(values):
    scale_rows = lax.rsqrt(lax.optimization_barrier(jnp.mean(values * values, axis=-1, keepdims=True)) + 1e-06)
    return (values * scale_rows / math.sqrt(values.shape[-1])).astype(jnp.bfloat16)

def reference(image_pooled, text_pooled, image_proj, text_proj, teacher_scale):
    image_unit = unit_rows(jnp.dot(image_pooled, image_proj, preferred_element_type=jnp.float32))
    text_unit = unit_rows(jnp.dot(text_pooled, text_proj, preferred_element_type=jnp.float32))
    logits = teacher_scale[0] * jnp.dot(image_unit, text_unit.T, preferred_element_type=jnp.float32)
    row_top = lax.optimization_barrier(jnp.max(logits, axis=1, keepdims=True))
    row_lse = row_top + jnp.log(lax.optimization_barrier(jnp.sum(jnp.exp(logits - row_top), axis=1, keepdims=True)))
    col_top = lax.optimization_barrier(jnp.max(logits, axis=0, keepdims=True))
    col_lse = col_top + jnp.log(lax.optimization_barrier(jnp.sum(jnp.exp(logits - col_top), axis=0, keepdims=True)))
    return (logits - row_lse, logits - col_lse)
```

```python
import math

import jax
import jax.numpy as jnp
from jax import lax
from jax.sharding import Mesh, PartitionSpec as P

SIZES = {"z": 8, "x": 4, "y": 4, "core": 2}
IMG = ("z", "x")
TXT = ("y", "core")
ROWS_A = 768


def shift(value, axis, step):
    count = SIZES[axis]
    return lax.ppermute(value, axis, [(i, (i + step) % count) for i in range(count)])


def unit_rows(values):
    scale_rows = lax.rsqrt(jnp.mean(values * values, axis=-1, keepdims=True) + 1e-06)
    return (values * scale_rows / math.sqrt(values.shape[-1])).astype(jnp.bfloat16)


def along_x(block):
    return [block, shift(block, "x", 1), shift(block, "x", -1), shift(block, "x", 2)]


def along_x_forwarding(block):
    half = block.shape[0] // 2
    ahead, back = shift(block, "x", 1), shift(block, "x", -1)
    far = [shift(ahead[:half], "x", 1), shift(back[half:], "x", -1)]
    return [block, ahead, back, jnp.concatenate(far, axis=0)]


def along_z(block, cut):
    ahead, back = [block], [block]
    for _ in range(3):
        ahead.append(shift(ahead[-1], "z", 1))
        back.append(shift(back[-1], "z", -1))
    half = block.shape[cut] // 2
    first = lax.slice_in_dim(ahead[3], 0, half, axis=cut)
    second = lax.slice_in_dim(back[3], half, 2 * half, axis=cut)
    far = jnp.concatenate([shift(first, "z", 1), shift(second, "z", -1)], axis=cut)
    return ahead + [far] + back[:0:-1]


def lse_over(local, axes, count):
    spread = jnp.broadcast_to(local[None], (count,) + local.shape)
    parts = lax.all_to_all(spread, axes, 0, 0)
    top = jnp.max(parts, axis=0)
    return top + jnp.log(jnp.sum(jnp.exp(parts - top), axis=0))


def on_device(image_pooled, text_pooled, image_proj, text_proj, teacher_scale):
    core = lax.axis_index("core")
    width = text_proj.shape[1] // 2
    text_lines = text_pooled.T
    own = lax.dynamic_slice_in_dim(text_proj, core * width, width, axis=1)
    block_a = jnp.concatenate([text_lines[:, :ROWS_A], own], axis=1)
    block_b = text_lines[:, ROWS_A:]

    partial = jnp.dot(image_pooled, image_proj, preferred_element_type=jnp.float32)
    image_part = lax.psum_scatter(partial, TXT, scatter_dimension=0, tiled=True)
    image_unit = lax.all_gather(unit_rows(image_part), TXT, axis=0, tiled=True)

    full_a = jnp.concatenate(along_z(jnp.concatenate(along_x(block_a), axis=0), 0), axis=0)
    full_b = jnp.concatenate(along_x_forwarding(jnp.concatenate(along_z(block_b, 1), axis=0)), axis=0)
    depth, rest = text_lines.shape[0], block_b.shape[1]
    full_b = full_b.reshape(4, 8, depth, rest).transpose(1, 0, 2, 3).reshape(32 * depth, rest)
    weight_own = full_a[:, ROWS_A:]
    weight = jnp.concatenate([weight_own, shift(weight_own, "core", 1)], axis=1)
    text_full = jnp.concatenate([full_a[:, :ROWS_A], full_b], axis=1)
    text_sum = lax.dot_general(
        text_full, weight, (((0,), (0,)), ((), ())), preferred_element_type=jnp.float32
    )
    text_unit = unit_rows(text_sum)
    image_unit = jnp.where(core == 0, image_unit, jnp.roll(image_unit, width, axis=1))
    similar = lax.dot_general(
        image_unit, text_unit, (((1,), (1,)), ((), ())), preferred_element_type=jnp.float32
    )
    logits = teacher_scale[0] * similar
    row_top = jnp.max(logits, axis=1)
    col_top = jnp.max(logits, axis=0)
    row_part = row_top + jnp.log(jnp.sum(jnp.exp(logits - row_top[:, None]), axis=1))
    col_part = col_top + jnp.log(jnp.sum(jnp.exp(logits - col_top[None, :]), axis=0))
    row_lse = lse_over(row_part.reshape(4, 128), TXT, 8).reshape(-1)
    col_lse = lse_over(col_part.reshape(16, 128), IMG, 32).reshape(-1)
    return (logits - row_lse[:, None], logits - col_lse[None, :])


def solution(mesh):
    grid = Mesh(mesh.devices.reshape(8, 4, 4, 2), ("z", "x", "y", "core"))
    placed = (P(IMG, TXT), P(TXT, IMG), P(TXT, None), P(IMG, None), P())
    return jax.shard_map(
        on_device,
        mesh=grid,
        in_specs=placed,
        out_specs=(P(IMG, TXT), P(IMG, TXT)),
        check_vma=False,
    )
```

```python
import functools
import math

import jax
import jax.numpy as jnp
from jax import lax
from jax.experimental import pallas as pl
from jax.experimental.pallas import tpu as pltpu
from jax.sharding import Mesh, PartitionSpec as P

SIZES = {"z": 8, "x": 4, "y": 4, "core": 2}
IMG = ("z", "x")
TXT = ("y", "core")
ROWS_A = 768
TILE_B = 640
VMEM_LIMIT = 24 * 1024 * 1024
BUSY = pl.CostEstimate(flops=10**10, bytes_accessed=10**7, transcendentals=0)


def shift(value, axis, step):
    count = SIZES[axis]
    return lax.ppermute(value, axis, [(i, (i + step) % count) for i in range(count)])


def after(value, *others):
    return lax.optimization_barrier((value, *others))[0]


def together(*values):
    return lax.optimization_barrier(values)


def params():
    return pltpu.CompilerParams(vmem_limit_bytes=VMEM_LIMIT)


def whole():
    return pl.BlockSpec(memory_space=pltpu.VMEM)


def fixed(*shape):
    return pl.BlockSpec(shape, lambda j: (0,) * len(shape), pipeline_mode=pl.Buffered(1))


def from_hbm(values):
    return [pltpu.with_memory_space_constraint(value, pltpu.HBM) for value in values]


def anywhere(count):
    return [pl.BlockSpec(memory_space=pl.ANY)] * count


def fetch(pairs, sem):
    copies = [pltpu.make_async_copy(source, target, sem.at[i]) for i, (source, target) in enumerate(pairs)]
    for copy in copies:
        copy.start()
    return copies


def join_kernel(*refs):
    *blocks, joined, lines, sem = refs
    depth = blocks[0].shape[0]
    copies = fetch([(block, lines.at[i]) for i, block in enumerate(blocks)], sem)
    for i, copy in enumerate(copies):
        copy.wait()
        joined[i * depth : (i + 1) * depth, :] = lines[i]


def join(blocks):
    depth, width = blocks[0].shape
    return pl.pallas_call(
        join_kernel,
        out_shape=jax.ShapeDtypeStruct((len(blocks) * depth, width), jnp.bfloat16),
        in_specs=anywhere(len(blocks)),
        out_specs=whole(),
        scratch_shapes=[
            pltpu.VMEM((len(blocks), depth, width), jnp.bfloat16),
            pltpu.SemaphoreType.DMA((len(blocks),)),
        ],
        compiler_params=params(),
        name="join",
    )(*from_hbm(blocks))


def in_turn(own, ahead, back):
    order = [own]
    for pair in zip(ahead, back):
        order += pair
    return order


def place(chunk, position, depth, features, weight):
    for i in range(4):
        at, to = i * depth, (i * 8 + position) * depth
        features[to : to + depth, :] = chunk[at : at + depth, :ROWS_A]
        weight[to : to + depth, :] = chunk[at : at + depth, ROWS_A:]


def split_kernel(depth, *refs):
    *chunks, features, weight, lines, sem = refs
    copies = fetch([(chunk, lines.at[i]) for i, chunk in enumerate(chunks)], sem)
    for i, copy in enumerate(copies):
        copy.wait()
        place(lines.at[i], i, depth, features, weight)


def split_chunks(chunks, depth):
    width = chunks[0].shape[1]
    return pl.pallas_call(
        functools.partial(split_kernel, depth),
        out_shape=(
            jax.ShapeDtypeStruct((32 * depth, ROWS_A), jnp.bfloat16),
            jax.ShapeDtypeStruct((32 * depth, width - ROWS_A), jnp.bfloat16),
        ),
        in_specs=anywhere(len(chunks)),
        out_specs=(whole(), whole()),
        scratch_shapes=[
            pltpu.VMEM((len(chunks), 4 * depth, width), jnp.bfloat16),
            pltpu.SemaphoreType.DMA((len(chunks),)),
        ],
        compiler_params=params(),
        name="split_chunks",
        cost_estimate=BUSY,
    )(*from_hbm(chunks))


def image_kernel(rows, own, other, unit):
    total = None
    for lines in (own, other):
        part = lax.dot_general(
            lines[:, :rows],
            lines[:, rows:],
            (((0,), (0,)), ((), ())),
            preferred_element_type=jnp.float32,
        )
        total = part if total is None else total + part
    count = total.shape[1]
    mean = jnp.sum(total * total, axis=1, keepdims=True) / count
    unit[...] = (total * (lax.rsqrt(mean + 1e-06) / math.sqrt(count))).astype(jnp.bfloat16)


def image_units(rows, own, other):
    return pl.pallas_call(
        functools.partial(image_kernel, rows),
        out_shape=jax.ShapeDtypeStruct((rows, own.shape[1] - rows), jnp.bfloat16),
        grid=(1,),
        in_specs=[fixed(*own.shape), fixed(*own.shape)],
        out_specs=fixed(rows, own.shape[1] - rows),
        compiler_params=params(),
        name="image_units",
        cost_estimate=BUSY,
    )(own, other)


def lanes(value):
    return [value[:, at : at + 128] for at in range(0, value.shape[1], 128)]


def score_tile(scale, weight, image, features, logits, col_part, top, total):
    text_sum = jnp.dot(weight, features, preferred_element_type=jnp.float32)
    count = text_sum.shape[0]
    mean = jnp.sum(text_sum * text_sum, axis=0, keepdims=True) / count
    unit = (text_sum * (lax.rsqrt(mean + 1e-06) / math.sqrt(count))).astype(jnp.bfloat16)
    block = scale[0] * jnp.dot(image, unit, preferred_element_type=jnp.float32)
    logits[...] = block
    col_top = jnp.max(block, axis=0, keepdims=True)
    col_part[...] = col_top + jnp.log(jnp.sum(jnp.exp(block - col_top), axis=0, keepdims=True))
    groups = lanes(block)
    old_top = top[...]
    new_top = functools.reduce(jnp.maximum, groups, old_top)
    fresh = sum(jnp.exp(group - new_top) for group in groups)
    total[...] = total[...] * jnp.exp(old_top - new_top) + fresh
    top[...] = new_top


def score_kernel(depth, core, scale, own, other, far_own, far_other, image, text_a, *refs):
    chunks_b, (logits, col_part, row_part, *scratch) = refs[:5], refs[5:]
    own_in, other_in, far_in, image_in, a_in, b_in, weight, logits_a, logits_b, top, total, sem = scratch
    pairs = [(own, own_in), (far_own, far_in.at[0]), (other, other_in), (far_other, far_in.at[1])]
    pairs += [(text_a, a_in), (image, image_in)]
    at = 0
    for chunk in chunks_b:
        pairs.append((chunk, b_in.at[pl.ds(at, chunk.shape[0]), :]))
        at += chunk.shape[0]
    arriving = fetch(pairs, sem)
    top[...] = jnp.full_like(top, -1e30)
    total[...] = jnp.zeros_like(total)
    half = own.shape[1]
    for copy in arriving[:2]:
        copy.wait()
    arriving[4].wait()
    place(far_in.at[0], 7, depth, a_in, own_in)
    weight[pl.ds(pl.multiple_of(core[0] * half, half), half), :] = own_in[...].T
    for copy in arriving[2:4]:
        copy.wait()
    for i in range(4):
        at, to = i * depth, (i * 8 + 7) * depth
        other_in[to : to + depth, :] = far_in[1, at : at + depth, ROWS_A:]
    weight[pl.ds(pl.multiple_of((1 - core[0]) * half, half), half), :] = other_in[...].T
    arriving[5].wait()
    tiles = [(a_in, 0, a_in.shape[1], logits_a)]
    tiles += [(b_in, i * TILE_B, TILE_B, logits_b.at[i]) for i in range(b_in.shape[1] // TILE_B)]
    leaving, to = [], 0
    for i, (text, at, count, block) in enumerate(tiles):
        if i == 1:
            for copy in arriving[6:]:
                copy.wait()
        here = pl.ds(to, count)
        score_tile(
            scale, weight[...], image_in[...], text[:, pl.ds(at, count)], block, col_part.at[:, here], top, total
        )
        leaving.append(pltpu.make_async_copy(block, logits.at[:, here], sem.at[len(pairs) + i]))
        leaving[-1].start()
        to += count
    row_top = jnp.max(top[...], axis=1, keepdims=True)
    row_sum = jnp.sum(total[...] * jnp.exp(top[...] - row_top), axis=1, keepdims=True)
    row_part[...] = row_top + jnp.log(row_sum)
    for copy in leaving:
        copy.wait()


def score(depth, core, scale, own, other, far_own, far_other, image, text_a, chunks_b):
    rows, count = image.shape
    width_a, width_b = text_a.shape[1], chunks_b[0].shape[1]
    columns = width_a + width_b
    smem = pl.BlockSpec(memory_space=pltpu.SMEM)
    values = [own, other, far_own, far_other, image, text_a, *chunks_b]
    return pl.pallas_call(
        functools.partial(score_kernel, depth),
        out_shape=(
            pltpu.HBM((rows, columns), jnp.float32),
            jax.ShapeDtypeStruct((1, columns), jnp.float32),
            jax.ShapeDtypeStruct((rows, 1), jnp.float32),
        ),
        in_specs=[smem, smem] + anywhere(len(values)),
        out_specs=(pl.BlockSpec(memory_space=pltpu.HBM), whole(), whole()),
        scratch_shapes=[
            pltpu.VMEM(own.shape, jnp.bfloat16),
            pltpu.VMEM(own.shape, jnp.bfloat16),
            pltpu.VMEM((2, *far_own.shape), jnp.bfloat16),
            pltpu.VMEM(image.shape, jnp.bfloat16),
            pltpu.VMEM(text_a.shape, jnp.bfloat16),
            pltpu.VMEM((own.shape[0], width_b), jnp.bfloat16),
            pltpu.VMEM((count, own.shape[0]), jnp.bfloat16),
            pltpu.VMEM((rows, width_a), jnp.float32),
            pltpu.VMEM((width_b // TILE_B, rows, TILE_B), jnp.float32),
            pltpu.VMEM((rows, 128), jnp.float32),
            pltpu.VMEM((rows, 128), jnp.float32),
            pltpu.SemaphoreType.DMA((len(values) + 1 + width_b // TILE_B,)),
        ],
        compiler_params=pltpu.CompilerParams(vmem_limit_bytes=44 * 1024 * 1024),
        name="score",
    )(core, scale, *from_hbm(values))


def minus_kernel(logits, lse, out, lines, sem_in, sem_out):
    count, tall, _ = lines.shape
    parts = [pl.ds(i * tall, tall) for i in range(count)]
    arriving = fetch([(logits.at[here, :], lines.at[i]) for i, here in enumerate(parts)], sem_in)
    leaving = []
    for i, here in enumerate(parts):
        arriving[i].wait()
        lines[i] = lines[i] - (lse[...] if lse.shape[0] == 1 else lse[here, :])
        leaving.append(pltpu.make_async_copy(lines.at[i], out.at[here, :], sem_out.at[i]))
        leaving[-1].start()
    for copy in leaving:
        copy.wait()


def minus(logits, lse):
    rows, columns = logits.shape
    parts = 8
    return pl.pallas_call(
        minus_kernel,
        out_shape=pltpu.HBM((rows, columns), jnp.float32),
        in_specs=[pl.BlockSpec(memory_space=pl.ANY), whole()],
        out_specs=pl.BlockSpec(memory_space=pltpu.HBM),
        scratch_shapes=[
            pltpu.VMEM((parts, rows // parts, columns), jnp.float32),
            pltpu.SemaphoreType.DMA((parts,)),
            pltpu.SemaphoreType.DMA((parts,)),
        ],
        compiler_params=params(),
        name="minus",
    )(*from_hbm([logits]), lse)


def add_exp(parts):
    top = jnp.max(parts, axis=0)
    return top + jnp.log(jnp.sum(jnp.exp(parts - top), axis=0))


def on_device(image_pooled, text_pooled, image_proj, text_proj, teacher_scale):
    core = lax.axis_index("core")
    width = text_proj.shape[1] // 2
    rows = image_pooled.shape[0]
    text_lines = text_pooled.T
    depth, columns = text_lines.shape
    own = lax.dynamic_slice_in_dim(text_proj, core * width, width, axis=1)

    block_a = jnp.concatenate([text_lines[:, :ROWS_A], own], axis=1)
    block_b = text_lines[:, ROWS_A:]
    image_lines = jnp.concatenate([image_pooled.T, image_proj], axis=1)

    ahead_b, back_b = [shift(block_b, "z", 1)], [shift(block_b, "z", -1)]
    block_a = join([block_a] + [shift(block_a, "x", step) for step in (1, -1, 2)])
    block_a, ahead_b[0], back_b[0], image_lines = together(block_a, ahead_b[0], back_b[0], image_lines)

    ahead_a, back_a = [shift(block_a, "z", 1)], [shift(block_a, "z", -1)]
    ahead_b.append(shift(ahead_b[0], "z", 1))
    back_b.append(shift(back_b[0], "z", -1))
    spread = jnp.broadcast_to(image_lines[None], (SIZES["y"],) + image_lines.shape)
    image_own = lax.all_to_all(spread, "y", 0, 0).reshape(-1, image_lines.shape[1])
    ahead_a[0], back_a[0], ahead_b[1], back_b[1] = together(ahead_a[0], back_a[0], ahead_b[1], back_b[1])

    ahead_a.append(shift(ahead_a[0], "z", 1))
    back_a.append(shift(back_a[0], "z", -1))
    ahead_b.append(shift(ahead_b[1], "z", 1))
    back_b.append(shift(back_b[1], "z", -1))
    far_b = shift(ahead_b[2], "z", 1)
    block_b = jnp.concatenate(in_turn(block_b, ahead_b, back_b) + [far_b], axis=0)
    ahead_a[1], back_a[1], block_b = together(ahead_a[1], back_a[1], block_b)

    ahead_a.append(shift(ahead_a[1], "z", 1))
    back_a.append(shift(back_a[1], "z", -1))
    ahead_x, back_x = shift(block_b, "x", 1), shift(block_b, "x", -1)
    half = block_b.shape[0] // 2
    ahead_a[2], back_a[2], from_ahead, from_back, image_own = together(
        ahead_a[2], back_a[2], ahead_x[:half], back_x[half:], image_own
    )

    far_a = shift(ahead_a[2], "z", 1)
    far_x = [shift(from_ahead, "x", 1), shift(from_back, "x", -1)]
    image_other = shift(image_own, "core", 1)
    image_unit = image_units(rows, image_own, image_other)

    text_a, weight_own = split_chunks(in_turn(block_a, ahead_a, back_a), depth)
    weight_other = shift(weight_own, "core", 1)
    far_a = after(far_a, weight_other, image_unit, *far_x)
    far_other = shift(far_a, "core", 1)
    chunks_b = [block_b, ahead_x, back_x, *far_x]
    logits, col_part, row_part = score(
        depth, core.reshape(1), teacher_scale, weight_own, weight_other, far_a, far_other, image_unit, text_a, chunks_b
    )
    col_part = col_part.reshape(columns // 128, 128)
    spread = jnp.broadcast_to(col_part[None], (32,) + col_part.shape)
    col_lse = add_exp(lax.all_to_all(spread, IMG, 0, 0)).reshape(-1)

    row_part = row_part.reshape(rows // 128, 128)
    row_part = add_exp(jnp.stack([row_part, shift(row_part, "core", 1)]))
    row_parts = [row_part] + [shift(row_part, "y", step) for step in (1, -1, 2)]
    row_lse = add_exp(jnp.stack(row_parts)).reshape(-1)
    image_targets = minus(logits, row_lse[:, None])
    text_targets = minus(logits, col_lse[None, :])
    return (image_targets, text_targets)


def solution(mesh):
    grid = Mesh(mesh.devices.reshape(8, 4, 4, 2), ("z", "x", "y", "core"))
    placed = (P(IMG, TXT), P(TXT, IMG), P(TXT, None), P(IMG, None), P())
    return jax.shard_map(
        on_device,
        mesh=grid,
        in_specs=placed,
        out_specs=(P(IMG, TXT), P(IMG, TXT)),
        check_vma=False,
    )
```

```python
import functools
import math

import jax
import jax.numpy as jnp
from jax import lax
from jax.experimental import pallas as pl
from jax.experimental.pallas import tpu as pltpu
from jax.sharding import Mesh, PartitionSpec as P

SIZES = {"z": 8, "x": 4, "y": 4, "core": 2}
IMG = ("z", "x")
TXT = ("y", "core")
ROWS_A = 512
TILE = 512
VMEM_LIMIT = 24 * 1024 * 1024
BUSY = pl.CostEstimate(flops=10**10, bytes_accessed=10**7, transcendentals=0)


def shift(value, axis, step):
    count = SIZES[axis]
    return lax.ppermute(value, axis, [(i, (i + step) % count) for i in range(count)])


def after(value, *others):
    return lax.optimization_barrier((value, *others))[0]


def together(*values):
    return lax.optimization_barrier(values)


def params():
    return pltpu.CompilerParams(vmem_limit_bytes=VMEM_LIMIT)


def whole():
    return pl.BlockSpec(memory_space=pltpu.VMEM)


def fixed(*shape):
    return pl.BlockSpec(shape, lambda j: (0,) * len(shape), pipeline_mode=pl.Buffered(1))


def from_hbm(values):
    return [pltpu.with_memory_space_constraint(value, pltpu.HBM) for value in values]


def anywhere(count):
    return [pl.BlockSpec(memory_space=pl.ANY)] * count


def fetch(pairs, sem):
    copies = [pltpu.make_async_copy(source, target, sem.at[i]) for i, (source, target) in enumerate(pairs)]
    for copy in copies:
        copy.start()
    return copies


def join_kernel(*refs):
    *blocks, joined, lines, sem = refs
    depth = blocks[0].shape[0]
    copies = fetch([(block, lines.at[i]) for i, block in enumerate(blocks)], sem)
    for i, copy in enumerate(copies):
        copy.wait()
        joined[i * depth : (i + 1) * depth, :] = lines[i]


def join(blocks):
    depth, width = blocks[0].shape
    return pl.pallas_call(
        join_kernel,
        out_shape=jax.ShapeDtypeStruct((len(blocks) * depth, width), jnp.bfloat16),
        in_specs=anywhere(len(blocks)),
        out_specs=whole(),
        scratch_shapes=[
            pltpu.VMEM((len(blocks), depth, width), jnp.bfloat16),
            pltpu.SemaphoreType.DMA((len(blocks),)),
        ],
        compiler_params=params(),
        name="join",
    )(*from_hbm(blocks))


def in_turn(own, ahead, back):
    order = [own]
    for pair in zip(ahead, back):
        order += pair
    return order


def place(chunk, position, depth, features, weight):
    for i in range(4):
        at, to = i * depth, (i * 8 + position) * depth
        features[to : to + depth, :] = chunk[at : at + depth, :ROWS_A]
        weight[to : to + depth, :] = chunk[at : at + depth, ROWS_A:]


def split_kernel(depth, *refs):
    *chunks, features, weight, lines, sem = refs
    copies = fetch([(chunk, lines.at[i]) for i, chunk in enumerate(chunks)], sem)
    for i, copy in enumerate(copies):
        copy.wait()
        place(lines.at[i], i, depth, features, weight)


def split_chunks(chunks, depth):
    width = chunks[0].shape[1]
    return pl.pallas_call(
        functools.partial(split_kernel, depth),
        out_shape=(
            jax.ShapeDtypeStruct((32 * depth, ROWS_A), jnp.bfloat16),
            jax.ShapeDtypeStruct((32 * depth, width - ROWS_A), jnp.bfloat16),
        ),
        in_specs=anywhere(len(chunks)),
        out_specs=(whole(), whole()),
        scratch_shapes=[
            pltpu.VMEM((len(chunks), 4 * depth, width), jnp.bfloat16),
            pltpu.SemaphoreType.DMA((len(chunks),)),
        ],
        compiler_params=params(),
        name="split_chunks",
        cost_estimate=BUSY,
    )(*from_hbm(chunks))


def image_kernel(rows, own, other, unit):
    total = None
    for lines in (own, other):
        part = lax.dot_general(
            lines[:, :rows],
            lines[:, rows:],
            (((0,), (0,)), ((), ())),
            preferred_element_type=jnp.float32,
        )
        total = part if total is None else total + part
    count = total.shape[1]
    mean = jnp.sum(total * total, axis=1, keepdims=True) / count
    unit[...] = (total * (lax.rsqrt(mean + 1e-06) / math.sqrt(count))).astype(jnp.bfloat16)


def image_units(rows, own, other):
    return pl.pallas_call(
        functools.partial(image_kernel, rows),
        out_shape=jax.ShapeDtypeStruct((rows, own.shape[1] - rows), jnp.bfloat16),
        grid=(1,),
        in_specs=[fixed(*own.shape), fixed(*own.shape)],
        out_specs=fixed(rows, own.shape[1] - rows),
        compiler_params=params(),
        name="image_units",
        cost_estimate=BUSY,
    )(own, other)


def lanes(value):
    return [value[:, at : at + 128] for at in range(0, value.shape[1], 128)]


def score_tile(scale, weight, image, features, logits, col_part, top, total):
    text_sum = jnp.dot(weight, features, preferred_element_type=jnp.float32)
    count = text_sum.shape[0]
    mean = jnp.sum(text_sum * text_sum, axis=0, keepdims=True) / count
    unit = (text_sum * (lax.rsqrt(mean + 1e-06) / math.sqrt(count))).astype(jnp.bfloat16)
    block = scale[0] * jnp.dot(image, unit, preferred_element_type=jnp.float32)
    logits[...] = block
    col_top = jnp.max(block, axis=0, keepdims=True)
    col_part[...] = col_top + jnp.log(jnp.sum(jnp.exp(block - col_top), axis=0, keepdims=True))
    groups = lanes(block)
    old_top = top[...]
    new_top = functools.reduce(jnp.maximum, groups, old_top)
    fresh = sum(jnp.exp(group - new_top) for group in groups)
    total[...] = total[...] * jnp.exp(old_top - new_top) + fresh
    top[...] = new_top


def tiles_of(text):
    columns = text.shape[1]
    return [(text, at, min(TILE, columns - at)) for at in range(0, columns, TILE)]


def score_kernel(depth, core, scale, own, other, far_own, far_other, image, text_a, *refs):
    chunks_b, (logits, col_part, row_part, *scratch) = refs[:5], refs[5:]
    own_in, other_in, far_in, image_in, a_in, b_in, weight, logits_in, top, total, sem = scratch
    pairs = [(own, own_in), (far_own, far_in.at[0]), (other, other_in), (far_other, far_in.at[1])]
    pairs += [(text_a, a_in), (image, image_in)]
    at = 0
    for chunk in chunks_b:
        pairs.append((chunk, b_in.at[pl.ds(at, chunk.shape[0]), :]))
        at += chunk.shape[0]
    arriving = fetch(pairs, sem)
    top[...] = jnp.full_like(top, -1e30)
    total[...] = jnp.zeros_like(total)
    half = own.shape[1]
    for copy in arriving[:2]:
        copy.wait()
    arriving[4].wait()
    place(far_in.at[0], 7, depth, a_in, own_in)
    weight[pl.ds(pl.multiple_of(core[0] * half, half), half), :] = own_in[...].T
    for copy in arriving[2:4]:
        copy.wait()
    for i in range(4):
        at, to = i * depth, (i * 8 + 7) * depth
        other_in[to : to + depth, :] = far_in[1, at : at + depth, ROWS_A:]
    weight[pl.ds(pl.multiple_of((1 - core[0]) * half, half), half), :] = other_in[...].T
    arriving[5].wait()
    tiles = tiles_of(a_in) + tiles_of(b_in)
    leaving, to = [], 0
    for i, (text, at, count) in enumerate(tiles):
        if text is b_in and at == 0:
            for copy in arriving[6:]:
                copy.wait()
        here = pl.ds(to, count)
        block = logits_in.at[:, here]
        score_tile(
            scale, weight[...], image_in[...], text[:, pl.ds(at, count)], block, col_part.at[:, here], top, total
        )
        leaving.append(pltpu.make_async_copy(block, logits.at[:, here], sem.at[len(pairs) + i]))
        leaving[-1].start()
        to += count
    row_top = jnp.max(top[...], axis=1, keepdims=True)
    row_sum = jnp.sum(total[...] * jnp.exp(top[...] - row_top), axis=1, keepdims=True)
    row_part[...] = row_top + jnp.log(row_sum)
    for copy in leaving:
        copy.wait()


def score(depth, core, scale, own, other, far_own, far_other, image, text_a, chunks_b):
    rows, count = image.shape
    width_a, width_b = text_a.shape[1], chunks_b[0].shape[1]
    columns = width_a + width_b
    smem = pl.BlockSpec(memory_space=pltpu.SMEM)
    values = [own, other, far_own, far_other, image, text_a, *chunks_b]
    return pl.pallas_call(
        functools.partial(score_kernel, depth),
        out_shape=(
            pltpu.HBM((rows, columns), jnp.float32),
            jax.ShapeDtypeStruct((1, columns), jnp.float32),
            jax.ShapeDtypeStruct((rows, 1), jnp.float32),
        ),
        in_specs=[smem, smem] + anywhere(len(values)),
        out_specs=(pl.BlockSpec(memory_space=pltpu.HBM), whole(), whole()),
        scratch_shapes=[
            pltpu.VMEM(own.shape, jnp.bfloat16),
            pltpu.VMEM(own.shape, jnp.bfloat16),
            pltpu.VMEM((2, *far_own.shape), jnp.bfloat16),
            pltpu.VMEM(image.shape, jnp.bfloat16),
            pltpu.VMEM(text_a.shape, jnp.bfloat16),
            pltpu.VMEM((own.shape[0], width_b), jnp.bfloat16),
            pltpu.VMEM((count, own.shape[0]), jnp.bfloat16),
            pltpu.VMEM((rows, columns), jnp.float32),
            pltpu.VMEM((rows, 128), jnp.float32),
            pltpu.VMEM((rows, 128), jnp.float32),
            pltpu.SemaphoreType.DMA((len(values) + columns // TILE + 2,)),
        ],
        compiler_params=pltpu.CompilerParams(vmem_limit_bytes=44 * 1024 * 1024),
        name="score",
    )(core, scale, own, other, far_own, far_other, image, text_a, *from_hbm(chunks_b[:3]), *chunks_b[3:])


def minus_kernel(logits, lse, out, lines, sem_in, sem_out):
    count, tall, _ = lines.shape
    parts = [pl.ds(i * tall, tall) for i in range(count)]
    arriving = fetch([(logits.at[here, :], lines.at[i]) for i, here in enumerate(parts)], sem_in)
    leaving = []
    for i, here in enumerate(parts):
        arriving[i].wait()
        lines[i] = lines[i] - (lse[...] if lse.shape[0] == 1 else lse[here, :])
        leaving.append(pltpu.make_async_copy(lines.at[i], out.at[here, :], sem_out.at[i]))
        leaving[-1].start()
    for copy in leaving:
        copy.wait()


def minus(logits, lse):
    rows, columns = logits.shape
    parts = 8
    return pl.pallas_call(
        minus_kernel,
        out_shape=pltpu.HBM((rows, columns), jnp.float32),
        in_specs=[pl.BlockSpec(memory_space=pl.ANY), whole()],
        out_specs=pl.BlockSpec(memory_space=pltpu.HBM),
        scratch_shapes=[
            pltpu.VMEM((parts, rows // parts, columns), jnp.float32),
            pltpu.SemaphoreType.DMA((parts,)),
            pltpu.SemaphoreType.DMA((parts,)),
        ],
        compiler_params=params(),
        name="minus",
    )(*from_hbm([logits]), lse)


def add_exp(parts):
    top = jnp.max(parts, axis=0)
    return top + jnp.log(jnp.sum(jnp.exp(parts - top), axis=0))


def on_device(image_pooled, text_pooled, image_proj, text_proj, teacher_scale):
    core = lax.axis_index("core")
    width = text_proj.shape[1] // 2
    rows = image_pooled.shape[0]
    text_lines = text_pooled.T
    depth, columns = text_lines.shape
    own = lax.dynamic_slice_in_dim(text_proj, core * width, width, axis=1)

    block_a = jnp.concatenate([text_lines[:, :ROWS_A], own], axis=1)
    block_b = text_lines[:, ROWS_A:]
    image_lines = jnp.concatenate([image_pooled.T, image_proj], axis=1)

    ahead_b, back_b = [shift(block_b, "z", 1)], [shift(block_b, "z", -1)]
    block_a = join([block_a] + [shift(block_a, "x", step) for step in (1, -1, 2)])
    block_a, ahead_b[0], back_b[0], image_lines = together(block_a, ahead_b[0], back_b[0], image_lines)

    ahead_a, back_a = [shift(block_a, "z", 1)], [shift(block_a, "z", -1)]
    ahead_b.append(shift(ahead_b[0], "z", 1))
    back_b.append(shift(back_b[0], "z", -1))
    spread = jnp.broadcast_to(image_lines[None], (SIZES["y"],) + image_lines.shape)
    image_own = lax.all_to_all(spread, "y", 0, 0).reshape(-1, image_lines.shape[1])
    ahead_a[0], back_a[0], ahead_b[1], back_b[1] = together(ahead_a[0], back_a[0], ahead_b[1], back_b[1])

    ahead_a.append(shift(ahead_a[0], "z", 1))
    back_a.append(shift(back_a[0], "z", -1))
    ahead_b.append(shift(ahead_b[1], "z", 1))
    back_b.append(shift(back_b[1], "z", -1))
    far_b = shift(ahead_b[2], "z", 1)
    blocks_b = [after(block_b, ahead_b[0])]
    for step in range(3):
        later = ahead_b[step + 1] if step < 2 else far_b
        blocks_b += [after(ahead_b[step], later), after(back_b[step], later)]
    block_b = jnp.concatenate(blocks_b + [far_b], axis=0)
    ahead_a[1], back_a[1], block_b = together(ahead_a[1], back_a[1], block_b)

    ahead_a.append(shift(ahead_a[1], "z", 1))
    back_a.append(shift(back_a[1], "z", -1))
    ahead_x, back_x = shift(block_b, "x", 1), shift(block_b, "x", -1)
    half = block_b.shape[0] // 2
    ahead_a[2], back_a[2], from_ahead, from_back, image_own = together(
        ahead_a[2], back_a[2], ahead_x[:half], back_x[half:], image_own
    )

    far_a = shift(ahead_a[2], "z", 1)
    far_x = [shift(from_ahead, "x", 1), shift(from_back, "x", -1)]
    image_other = shift(image_own, "core", 1)
    image_unit = image_units(rows, image_own, image_other)

    text_a, weight_own = split_chunks(in_turn(block_a, ahead_a, back_a), depth)
    weight_other = shift(weight_own, "core", 1)
    far_other = shift(far_a, "core", 1)
    chunks_b = [block_b, ahead_x, back_x, *far_x]
    logits, col_part, row_part = score(
        depth, core.reshape(1), teacher_scale, weight_own, weight_other, far_a, far_other, image_unit, text_a, chunks_b
    )
    col_part = col_part.reshape(columns // 128, 128)
    spread = jnp.broadcast_to(col_part[None], (32,) + col_part.shape)
    col_lse = add_exp(lax.all_to_all(spread, IMG, 0, 0)).reshape(-1)

    row_part = row_part.reshape(rows // 128, 128)
    row_part = add_exp(jnp.stack([row_part, shift(row_part, "core", 1)]))
    row_parts = [row_part] + [shift(row_part, "y", step) for step in (1, -1, 2)]
    row_lse = add_exp(jnp.stack(row_parts)).reshape(-1)
    image_targets = minus(logits, row_lse[:, None])
    text_targets = minus(logits, col_lse[None, :])
    return (image_targets, text_targets)


def solution(mesh):
    grid = Mesh(mesh.devices.reshape(8, 4, 4, 2), ("z", "x", "y", "core"))
    placed = (P(IMG, TXT), P(TXT, IMG), P(TXT, None), P(IMG, None), P())
    return jax.shard_map(
        on_device,
        mesh=grid,
        in_specs=placed,
        out_specs=(P(IMG, TXT), P(IMG, TXT)),
        check_vma=False,
    )
```

```python
import functools
import math

import jax
import jax.numpy as jnp
from jax import lax
from jax.experimental import pallas as pl
from jax.experimental.pallas import tpu as pltpu
from jax.sharding import Mesh, PartitionSpec as P

SIZES = {"z": 8, "x": 4, "y": 4, "core": 2}
IMG = ("z", "x")
TXT = ("y", "core")
ROWS_A = 512
TILE = 512
VMEM_LIMIT = 24 * 1024 * 1024
BUSY = pl.CostEstimate(flops=10**10, bytes_accessed=10**7, transcendentals=0)


def shift(value, axis, step):
    count = SIZES[axis]
    return lax.ppermute(value, axis, [(i, (i + step) % count) for i in range(count)])


def after(value, *others):
    return lax.optimization_barrier((value, *others))[0]


def together(*values):
    return lax.optimization_barrier(values)


def params():
    return pltpu.CompilerParams(vmem_limit_bytes=VMEM_LIMIT)


def whole():
    return pl.BlockSpec(memory_space=pltpu.VMEM)


def fixed(*shape):
    return pl.BlockSpec(shape, lambda j: (0,) * len(shape), pipeline_mode=pl.Buffered(1))


def from_hbm(values):
    return [pltpu.with_memory_space_constraint(value, pltpu.HBM) for value in values]


def anywhere(count):
    return [pl.BlockSpec(memory_space=pl.ANY)] * count


def fetch(pairs, sem):
    copies = [pltpu.make_async_copy(source, target, sem.at[i]) for i, (source, target) in enumerate(pairs)]
    for copy in copies:
        copy.start()
    return copies


def join_kernel(*refs):
    *blocks, joined, lines, sem = refs
    depth = blocks[0].shape[0]
    copies = fetch([(block, lines.at[i]) for i, block in enumerate(blocks)], sem)
    for i, copy in enumerate(copies):
        copy.wait()
        joined[i * depth : (i + 1) * depth, :] = lines[i]


def join(blocks):
    depth, width = blocks[0].shape
    return pl.pallas_call(
        join_kernel,
        out_shape=jax.ShapeDtypeStruct((len(blocks) * depth, width), jnp.bfloat16),
        in_specs=anywhere(len(blocks)),
        out_specs=whole(),
        scratch_shapes=[
            pltpu.VMEM((len(blocks), depth, width), jnp.bfloat16),
            pltpu.SemaphoreType.DMA((len(blocks),)),
        ],
        compiler_params=params(),
        name="join",
    )(*from_hbm(blocks))


def in_turn(own, ahead, back):
    order = [own]
    for pair in zip(ahead, back):
        order += pair
    return order


def place(chunk, position, depth, features, weight):
    for i in range(4):
        at, to = i * depth, (i * 8 + position) * depth
        features[to : to + depth, :] = chunk[at : at + depth, :ROWS_A]
        weight[to : to + depth, :] = chunk[at : at + depth, ROWS_A:]


def split_kernel(depth, *refs):
    *chunks, features, weight, lines, sem = refs
    copies = fetch([(chunk, lines.at[i]) for i, chunk in enumerate(chunks)], sem)
    for i, copy in enumerate(copies):
        copy.wait()
        place(lines.at[i], i, depth, features, weight)


def split_chunks(chunks, depth):
    width = chunks[0].shape[1]
    return pl.pallas_call(
        functools.partial(split_kernel, depth),
        out_shape=(
            jax.ShapeDtypeStruct((32 * depth, ROWS_A), jnp.bfloat16),
            jax.ShapeDtypeStruct((32 * depth, width - ROWS_A), jnp.bfloat16),
        ),
        in_specs=anywhere(len(chunks)),
        out_specs=(whole(), whole()),
        scratch_shapes=[
            pltpu.VMEM((len(chunks), 4 * depth, width), jnp.bfloat16),
            pltpu.SemaphoreType.DMA((len(chunks),)),
        ],
        compiler_params=params(),
        name="split_chunks",
        cost_estimate=BUSY,
    )(*from_hbm(chunks))


def image_kernel(rows, own, other, unit):
    total = None
    for lines in (own, other):
        part = lax.dot_general(
            lines[:, :rows],
            lines[:, rows:],
            (((0,), (0,)), ((), ())),
            preferred_element_type=jnp.float32,
        )
        total = part if total is None else total + part
    count = total.shape[1]
    mean = jnp.sum(total * total, axis=1, keepdims=True) / count
    unit[...] = (total * (lax.rsqrt(mean + 1e-06) / math.sqrt(count))).astype(jnp.bfloat16)


def image_units(rows, own, other):
    return pl.pallas_call(
        functools.partial(image_kernel, rows),
        out_shape=jax.ShapeDtypeStruct((rows, own.shape[1] - rows), jnp.bfloat16),
        grid=(1,),
        in_specs=[fixed(*own.shape), fixed(*own.shape)],
        out_specs=fixed(rows, own.shape[1] - rows),
        compiler_params=params(),
        name="image_units",
        cost_estimate=BUSY,
    )(own, other)


def lanes(value):
    return [value[:, at : at + 128] for at in range(0, value.shape[1], 128)]


def score_tile(scale, weight, image, features, logits, col_part, top, total):
    text_sum = jnp.dot(weight, features, preferred_element_type=jnp.float32)
    count = text_sum.shape[0]
    mean = jnp.sum(text_sum * text_sum, axis=0, keepdims=True) / count
    unit = (text_sum * (lax.rsqrt(mean + 1e-06) / math.sqrt(count))).astype(jnp.bfloat16)
    block = scale[0] * jnp.dot(image, unit, preferred_element_type=jnp.float32)
    logits[...] = block
    col_top = jnp.max(block, axis=0, keepdims=True)
    col_part[...] = col_top + jnp.log(jnp.sum(jnp.exp(block - col_top), axis=0, keepdims=True))
    groups = lanes(block)
    old_top = top[...]
    new_top = functools.reduce(jnp.maximum, groups, old_top)
    fresh = sum(jnp.exp(group - new_top) for group in groups)
    total[...] = total[...] * jnp.exp(old_top - new_top) + fresh
    top[...] = new_top


def tiles_of(text):
    columns = text.shape[1]
    return [(text, at, min(TILE, columns - at)) for at in range(0, columns, TILE)]


def score_kernel(depth, core, scale, own, other, far_own, far_other, image, text_a, *refs):
    low, high, (logits, col_part, row_part, *scratch) = refs[:4], refs[4:8], refs[8:]
    own_in, other_in, far_in, image_in, a_in, low_in, high_in, b_in, weight, logits_in, top, total, sem = scratch
    pairs = [(own, own_in), (far_own, far_in.at[0]), (other, other_in), (far_other, far_in.at[1])]
    pairs += [(text_a, a_in), (image, image_in)]
    for i in range(4):
        pairs += [(low[i], low_in.at[i]), (high[i], high_in.at[i])]
    arriving = fetch(pairs, sem)
    top[...] = jnp.full_like(top, -1e30)
    total[...] = jnp.zeros_like(total)
    half = own.shape[1]
    for copy in arriving[:2]:
        copy.wait()
    arriving[4].wait()
    place(far_in.at[0], 7, depth, a_in, own_in)
    weight[pl.ds(pl.multiple_of(core[0] * half, half), half), :] = own_in[...].T
    for copy in arriving[2:4]:
        copy.wait()
    for i in range(4):
        at, to = i * depth, (i * 8 + 7) * depth
        other_in[to : to + depth, :] = far_in[1, at : at + depth, ROWS_A:]
    weight[pl.ds(pl.multiple_of((1 - core[0]) * half, half), half), :] = other_in[...].T
    arriving[5].wait()
    tiles = tiles_of(a_in) + tiles_of(b_in)
    leaving, to = [], 0
    for i, (text, at, count) in enumerate(tiles):
        if text is b_in and at == 0:
            for copy in arriving[6:]:
                copy.wait()
            cut, tall = low_in.shape[1], 8 * depth
            for x in range(4):
                b_in[x * tall : x * tall + cut, :] = low_in[x]
                b_in[x * tall + cut : (x + 1) * tall, :] = high_in[x]
        here = pl.ds(to, count)
        block = logits_in.at[:, here]
        score_tile(
            scale, weight[...], image_in[...], text[:, pl.ds(at, count)], block, col_part.at[:, here], top, total
        )
        leaving.append(pltpu.make_async_copy(block, logits.at[:, here], sem.at[len(pairs) + i]))
        leaving[-1].start()
        to += count
    row_top = jnp.max(top[...], axis=1, keepdims=True)
    row_sum = jnp.sum(total[...] * jnp.exp(top[...] - row_top), axis=1, keepdims=True)
    row_part[...] = row_top + jnp.log(row_sum)
    for copy in leaving:
        copy.wait()


def score(depth, core, scale, own, other, far_own, far_other, image, text_a, low, high):
    rows, count = image.shape
    width_a, width_b = text_a.shape[1], low[0].shape[1]
    columns = width_a + width_b
    smem = pl.BlockSpec(memory_space=pltpu.SMEM)
    values = [own, other, far_own, far_other, image, text_a, *from_hbm(low[:3]), low[3], *from_hbm(high[:3]), high[3]]
    return pl.pallas_call(
        functools.partial(score_kernel, depth),
        out_shape=(
            pltpu.HBM((rows, columns), jnp.float32),
            jax.ShapeDtypeStruct((1, columns), jnp.float32),
            jax.ShapeDtypeStruct((rows, 1), jnp.float32),
        ),
        in_specs=[smem, smem] + anywhere(len(values)),
        out_specs=(pl.BlockSpec(memory_space=pltpu.HBM), whole(), whole()),
        scratch_shapes=[
            pltpu.VMEM(own.shape, jnp.bfloat16),
            pltpu.VMEM(own.shape, jnp.bfloat16),
            pltpu.VMEM((2, *far_own.shape), jnp.bfloat16),
            pltpu.VMEM(image.shape, jnp.bfloat16),
            pltpu.VMEM(text_a.shape, jnp.bfloat16),
            pltpu.VMEM((4, *low[0].shape), jnp.bfloat16),
            pltpu.VMEM((4, *high[0].shape), jnp.bfloat16),
            pltpu.VMEM((own.shape[0], width_b), jnp.bfloat16),
            pltpu.VMEM((count, own.shape[0]), jnp.bfloat16),
            pltpu.VMEM((rows, columns), jnp.float32),
            pltpu.VMEM((rows, 128), jnp.float32),
            pltpu.VMEM((rows, 128), jnp.float32),
            pltpu.SemaphoreType.DMA((len(values) + columns // TILE + 2,)),
        ],
        compiler_params=pltpu.CompilerParams(vmem_limit_bytes=44 * 1024 * 1024),
        name="score",
    )(core, scale, *values)


def minus_kernel(logits, lse, out, lines, sem_in, sem_out):
    count, tall, _ = lines.shape
    parts = [pl.ds(i * tall, tall) for i in range(count)]
    arriving = fetch([(logits.at[here, :], lines.at[i]) for i, here in enumerate(parts)], sem_in)
    leaving = []
    for i, here in enumerate(parts):
        arriving[i].wait()
        lines[i] = lines[i] - (lse[...] if lse.shape[0] == 1 else lse[here, :])
        leaving.append(pltpu.make_async_copy(lines.at[i], out.at[here, :], sem_out.at[i]))
        leaving[-1].start()
    for copy in leaving:
        copy.wait()


def minus(logits, lse):
    rows, columns = logits.shape
    parts = 8
    return pl.pallas_call(
        minus_kernel,
        out_shape=pltpu.HBM((rows, columns), jnp.float32),
        in_specs=[pl.BlockSpec(memory_space=pl.ANY), whole()],
        out_specs=pl.BlockSpec(memory_space=pltpu.HBM),
        scratch_shapes=[
            pltpu.VMEM((parts, rows // parts, columns), jnp.float32),
            pltpu.SemaphoreType.DMA((parts,)),
            pltpu.SemaphoreType.DMA((parts,)),
        ],
        compiler_params=params(),
        name="minus",
    )(*from_hbm([logits]), lse)


def add_exp(parts):
    top = jnp.max(parts, axis=0)
    return top + jnp.log(jnp.sum(jnp.exp(parts - top), axis=0))


def on_device(image_pooled, text_pooled, image_proj, text_proj, teacher_scale):
    core = lax.axis_index("core")
    width = text_proj.shape[1] // 2
    rows = image_pooled.shape[0]
    text_lines = text_pooled.T
    depth, columns = text_lines.shape
    own = lax.dynamic_slice_in_dim(text_proj, core * width, width, axis=1)

    block_a = jnp.concatenate([text_lines[:, :ROWS_A], own], axis=1)
    block_b = text_lines[:, ROWS_A:]
    image_lines = jnp.concatenate([image_pooled.T, image_proj], axis=1)

    ahead_b, back_b = [shift(block_b, "z", 1)], [shift(block_b, "z", -1)]
    block_a = join([block_a] + [shift(block_a, "x", step) for step in (1, -1, 2)])
    block_a, ahead_b[0], back_b[0], image_lines = together(block_a, ahead_b[0], back_b[0], image_lines)

    low = jnp.concatenate([block_b, ahead_b[0], back_b[0]], axis=0)
    ahead_low = shift(low, "x", 1)
    ahead_a, back_a = [shift(block_a, "z", 1)], [shift(block_a, "z", -1)]
    ahead_b.append(shift(ahead_b[0], "z", 1))
    back_b.append(shift(back_b[0], "z", -1))
    spread = jnp.broadcast_to(image_lines[None], (SIZES["y"],) + image_lines.shape)
    image_own = lax.all_to_all(spread, "y", 0, 0).reshape(-1, image_lines.shape[1])
    ahead_a[0], back_a[0], ahead_b[1], back_b[1], ahead_low = together(
        ahead_a[0], back_a[0], ahead_b[1], back_b[1], ahead_low
    )

    ahead_a.append(shift(ahead_a[0], "z", 1))
    back_a.append(shift(back_a[0], "z", -1))
    ahead_b.append(shift(ahead_b[1], "z", 1))
    back_b.append(shift(back_b[1], "z", -1))
    far_b = shift(ahead_b[2], "z", 1)
    back_low = shift(low, "x", -1)
    high = [after(ahead_b[1], ahead_b[2]), after(back_b[1], ahead_b[2])]
    high += [after(ahead_b[2], far_b), after(back_b[2], far_b), far_b]
    high = jnp.concatenate(high, axis=0)
    ahead_a[1], back_a[1], high, back_low = together(ahead_a[1], back_a[1], high, back_low)

    ahead_a.append(shift(ahead_a[1], "z", 1))
    back_a.append(shift(back_a[1], "z", -1))
    ahead_high, back_high = shift(high, "x", 1), shift(high, "x", -1)
    ahead_a[2], back_a[2], ahead_high, back_high, image_own = together(
        ahead_a[2], back_a[2], ahead_high, back_high, image_own
    )

    far_a = shift(ahead_a[2], "z", 1)
    far_low, far_high = shift(ahead_low, "x", 1), shift(back_high, "x", -1)
    image_other = shift(image_own, "core", 1)
    image_unit = image_units(rows, image_own, image_other)

    text_a, weight_own = split_chunks(in_turn(block_a, ahead_a, back_a), depth)
    weight_other = shift(weight_own, "core", 1)
    far_other = shift(far_a, "core", 1)
    lows = [low, ahead_low, back_low, far_low]
    highs = [high, ahead_high, back_high, far_high]
    logits, col_part, row_part = score(
        depth,
        core.reshape(1),
        teacher_scale,
        weight_own,
        weight_other,
        far_a,
        far_other,
        image_unit,
        text_a,
        lows,
        highs,
    )
    col_part = col_part.reshape(columns // 128, 128)
    spread = jnp.broadcast_to(col_part[None], (32,) + col_part.shape)
    col_lse = add_exp(lax.all_to_all(spread, IMG, 0, 0)).reshape(-1)

    row_part = row_part.reshape(rows // 128, 128)
    row_part = add_exp(jnp.stack([row_part, shift(row_part, "core", 1)]))
    row_parts = [row_part] + [shift(row_part, "y", step) for step in (1, -1, 2)]
    row_lse = add_exp(jnp.stack(row_parts)).reshape(-1)
    image_targets = minus(logits, row_lse[:, None])
    text_targets = minus(logits, col_lse[None, :])
    return (image_targets, text_targets)


def solution(mesh):
    grid = Mesh(mesh.devices.reshape(8, 4, 4, 2), ("z", "x", "y", "core"))
    placed = (P(IMG, TXT), P(TXT, IMG), P(TXT, None), P(IMG, None), P())
    return jax.shard_map(
        on_device,
        mesh=grid,
        in_specs=placed,
        out_specs=(P(IMG, TXT), P(IMG, TXT)),
        check_vma=False,
    )
```

```python
import functools
import math

import jax
import jax.numpy as jnp
from jax import lax
from jax.experimental import pallas as pl
from jax.experimental.pallas import tpu as pltpu
from jax.sharding import Mesh, PartitionSpec as P

SIZES = {"z": 8, "x": 4, "y": 4, "core": 2}
IMG = ("z", "x")
TXT = ("y", "core")
ROWS_A = 512
TILE = 512
VMEM_LIMIT = 24 * 1024 * 1024


def shift(value, axis, step):
    count = SIZES[axis]
    return lax.ppermute(value, axis, [(i, (i + step) % count) for i in range(count)])


def after(value, *others):
    return lax.optimization_barrier((value, *others))[0]


def together(*values):
    return lax.optimization_barrier(values)


def params():
    return pltpu.CompilerParams(vmem_limit_bytes=VMEM_LIMIT)


def whole():
    return pl.BlockSpec(memory_space=pltpu.VMEM)


def fixed(*shape):
    return pl.BlockSpec(shape, lambda j: (0,) * len(shape), pipeline_mode=pl.Buffered(1))


def from_hbm(values):
    return [pltpu.with_memory_space_constraint(value, pltpu.HBM) for value in values]


def anywhere(count):
    return [pl.BlockSpec(memory_space=pl.ANY)] * count


def fetch(pairs, sem):
    copies = [pltpu.make_async_copy(source, target, sem.at[i]) for i, (source, target) in enumerate(pairs)]
    for copy in copies:
        copy.start()
    return copies


def join_kernel(*refs):
    *blocks, joined, lines, sem = refs
    depth = blocks[0].shape[0]
    copies = fetch([(block, lines.at[i]) for i, block in enumerate(blocks)], sem)
    for i, copy in enumerate(copies):
        copy.wait()
        joined[i * depth : (i + 1) * depth, :] = lines[i]


def join(blocks):
    depth, width = blocks[0].shape
    return pl.pallas_call(
        join_kernel,
        out_shape=jax.ShapeDtypeStruct((len(blocks) * depth, width), jnp.bfloat16),
        in_specs=anywhere(len(blocks)),
        out_specs=whole(),
        scratch_shapes=[
            pltpu.VMEM((len(blocks), depth, width), jnp.bfloat16),
            pltpu.SemaphoreType.DMA((len(blocks),)),
        ],
        compiler_params=params(),
        name="join",
    )(*from_hbm(blocks))


def in_turn(own, ahead, back):
    order = [own]
    for pair in zip(ahead, back):
        order += pair
    return order


def place(chunk, position, depth, features, weight):
    for i in range(4):
        at, to = i * depth, (i * 8 + position) * depth
        features[to : to + depth, :] = chunk[at : at + depth, :ROWS_A]
        weight[to : to + depth, :] = chunk[at : at + depth, ROWS_A:]


def split_kernel(depth, *refs):
    *chunks, features, weight, lines, sem = refs
    copies = fetch([(chunk, lines.at[i]) for i, chunk in enumerate(chunks)], sem)
    for i, copy in enumerate(copies):
        copy.wait()
        place(lines.at[i], i, depth, features, weight)


def split_chunks(chunks, depth):
    width = chunks[0].shape[1]
    return pl.pallas_call(
        functools.partial(split_kernel, depth),
        out_shape=(
            jax.ShapeDtypeStruct((32 * depth, ROWS_A), jnp.bfloat16),
            jax.ShapeDtypeStruct((32 * depth, width - ROWS_A), jnp.bfloat16),
        ),
        in_specs=anywhere(len(chunks)),
        out_specs=(whole(), whole()),
        scratch_shapes=[
            pltpu.VMEM((len(chunks), 4 * depth, width), jnp.bfloat16),
            pltpu.SemaphoreType.DMA((len(chunks),)),
        ],
        compiler_params=params(),
        name="split_chunks",
    )(*from_hbm(chunks))


def image_kernel(rows, own, other, unit):
    total = None
    for lines in (own, other):
        part = lax.dot_general(
            lines[:, :rows],
            lines[:, rows:],
            (((0,), (0,)), ((), ())),
            preferred_element_type=jnp.float32,
        )
        total = part if total is None else total + part
    count = total.shape[1]
    mean = jnp.sum(total * total, axis=1, keepdims=True) / count
    unit[...] = (total * (lax.rsqrt(mean + 1e-06) / math.sqrt(count))).astype(jnp.bfloat16)


def image_units(rows, own, other):
    return pl.pallas_call(
        functools.partial(image_kernel, rows),
        out_shape=jax.ShapeDtypeStruct((rows, own.shape[1] - rows), jnp.bfloat16),
        grid=(1,),
        in_specs=[fixed(*own.shape), fixed(*own.shape)],
        out_specs=fixed(rows, own.shape[1] - rows),
        compiler_params=params(),
        name="image_units",
    )(own, other)


def lanes(value):
    return [value[:, at : at + 128] for at in range(0, value.shape[1], 128)]


def score_tile(scale, weight, image, features, logits, col_part, top, total):
    text_sum = jnp.dot(weight, features, preferred_element_type=jnp.float32)
    count = text_sum.shape[0]
    mean = jnp.sum(text_sum * text_sum, axis=0, keepdims=True) / count
    unit = (text_sum * (lax.rsqrt(mean + 1e-06) / math.sqrt(count))).astype(jnp.bfloat16)
    block = scale[0] * jnp.dot(image, unit, preferred_element_type=jnp.float32)
    logits[...] = block
    col_top = jnp.max(block, axis=0, keepdims=True)
    col_part[...] = col_top + jnp.log(jnp.sum(jnp.exp(block - col_top), axis=0, keepdims=True))
    groups = lanes(block)
    old_top = top[...]
    new_top = functools.reduce(jnp.maximum, groups, old_top)
    fresh = sum(jnp.exp(group - new_top) for group in groups)
    total[...] = total[...] * jnp.exp(old_top - new_top) + fresh
    top[...] = new_top


def tiles_of(text):
    columns = text.shape[1]
    return [(text, at, min(TILE, columns - at)) for at in range(0, columns, TILE)]


def score_kernel(depth, core, scale, own, other, far_own, far_other, image, text_a, *refs):
    low, high, (logits, col_part, row_part, *scratch) = refs[:4], refs[4:8], refs[8:]
    own_in, other_in, far_in, image_in, a_in, low_in, high_in, b_in, weight, logits_in, top, total, sem = scratch
    pairs = [(own, own_in), (far_own, far_in.at[0]), (other, other_in), (far_other, far_in.at[1])]
    pairs += [(text_a, a_in), (image, image_in)]
    for i in range(4):
        pairs += [(low[i], low_in.at[i]), (high[i], high_in.at[i])]
    arriving = fetch(pairs, sem)
    top[...] = jnp.full_like(top, -1e30)
    total[...] = jnp.zeros_like(total)
    half = own.shape[1]
    for copy in arriving[:2]:
        copy.wait()
    arriving[4].wait()
    place(far_in.at[0], 7, depth, a_in, own_in)
    weight[pl.ds(pl.multiple_of(core[0] * half, half), half), :] = own_in[...].T
    for copy in arriving[2:4]:
        copy.wait()
    for i in range(4):
        at, to = i * depth, (i * 8 + 7) * depth
        other_in[to : to + depth, :] = far_in[1, at : at + depth, ROWS_A:]
    weight[pl.ds(pl.multiple_of((1 - core[0]) * half, half), half), :] = other_in[...].T
    arriving[5].wait()
    tiles = tiles_of(a_in) + tiles_of(b_in)
    leaving, to = [], 0
    for i, (text, at, count) in enumerate(tiles):
        if text is b_in and at == 0:
            for copy in arriving[6:]:
                copy.wait()
            cut, tall = low_in.shape[1], 8 * depth
            for x in range(4):
                b_in[x * tall : x * tall + cut, :] = low_in[x]
                b_in[x * tall + cut : (x + 1) * tall, :] = high_in[x]
        here = pl.ds(to, count)
        block = logits_in.at[:, here]
        score_tile(
            scale, weight[...], image_in[...], text[:, pl.ds(at, count)], block, col_part.at[:, here], top, total
        )
        leaving.append(pltpu.make_async_copy(block, logits.at[:, here], sem.at[len(pairs) + i]))
        leaving[-1].start()
        to += count
    row_top = jnp.max(top[...], axis=1, keepdims=True)
    row_sum = jnp.sum(total[...] * jnp.exp(top[...] - row_top), axis=1, keepdims=True)
    row_part[...] = row_top + jnp.log(row_sum)
    for copy in leaving:
        copy.wait()


def score(depth, core, scale, own, other, far_own, far_other, image, text_a, low, high):
    rows, count = image.shape
    width_a, width_b = text_a.shape[1], low[0].shape[1]
    columns = width_a + width_b
    smem = pl.BlockSpec(memory_space=pltpu.SMEM)
    values = [own, other, far_own, far_other, image, text_a, *from_hbm(low[:3]), low[3], *from_hbm(high[:3]), high[3]]
    return pl.pallas_call(
        functools.partial(score_kernel, depth),
        out_shape=(
            pltpu.HBM((rows, columns), jnp.float32),
            jax.ShapeDtypeStruct((1, columns), jnp.float32),
            jax.ShapeDtypeStruct((rows, 1), jnp.float32),
        ),
        in_specs=[smem, smem] + anywhere(len(values)),
        out_specs=(pl.BlockSpec(memory_space=pltpu.HBM), whole(), whole()),
        scratch_shapes=[
            pltpu.VMEM(own.shape, jnp.bfloat16),
            pltpu.VMEM(own.shape, jnp.bfloat16),
            pltpu.VMEM((2, *far_own.shape), jnp.bfloat16),
            pltpu.VMEM(image.shape, jnp.bfloat16),
            pltpu.VMEM(text_a.shape, jnp.bfloat16),
            pltpu.VMEM((4, *low[0].shape), jnp.bfloat16),
            pltpu.VMEM((4, *high[0].shape), jnp.bfloat16),
            pltpu.VMEM((own.shape[0], width_b), jnp.bfloat16),
            pltpu.VMEM((count, own.shape[0]), jnp.bfloat16),
            pltpu.VMEM((rows, columns), jnp.float32),
            pltpu.VMEM((rows, 128), jnp.float32),
            pltpu.VMEM((rows, 128), jnp.float32),
            pltpu.SemaphoreType.DMA((len(values) + columns // TILE + 2,)),
        ],
        compiler_params=pltpu.CompilerParams(vmem_limit_bytes=44 * 1024 * 1024),
        name="score",
    )(core, scale, *values)


def minus_kernel(logits, lse, out, lines, sem_in, sem_out):
    count, tall, _ = lines.shape
    parts = [pl.ds(i * tall, tall) for i in range(count)]
    arriving = fetch([(logits.at[here, :], lines.at[i]) for i, here in enumerate(parts)], sem_in)
    leaving = []
    for i, here in enumerate(parts):
        arriving[i].wait()
        lines[i] = lines[i] - (lse[...] if lse.shape[0] == 1 else lse[here, :])
        leaving.append(pltpu.make_async_copy(lines.at[i], out.at[here, :], sem_out.at[i]))
        leaving[-1].start()
    for copy in leaving:
        copy.wait()


def minus(logits, lse):
    rows, columns = logits.shape
    parts = 8
    return pl.pallas_call(
        minus_kernel,
        out_shape=pltpu.HBM((rows, columns), jnp.float32),
        in_specs=[pl.BlockSpec(memory_space=pl.ANY), whole()],
        out_specs=pl.BlockSpec(memory_space=pltpu.HBM),
        scratch_shapes=[
            pltpu.VMEM((parts, rows // parts, columns), jnp.float32),
            pltpu.SemaphoreType.DMA((parts,)),
            pltpu.SemaphoreType.DMA((parts,)),
        ],
        compiler_params=params(),
        name="minus",
    )(*from_hbm([logits]), lse)


def add_exp(parts):
    top = jnp.max(parts, axis=0)
    return top + jnp.log(jnp.sum(jnp.exp(parts - top), axis=0))


def on_device(image_pooled, text_pooled, image_proj, text_proj, teacher_scale):
    core = lax.axis_index("core")
    width = text_proj.shape[1] // 2
    rows = image_pooled.shape[0]
    text_lines = text_pooled.T
    depth, columns = text_lines.shape
    own = lax.dynamic_slice_in_dim(text_proj, core * width, width, axis=1)

    block_a = jnp.concatenate([text_lines[:, :ROWS_A], own], axis=1)
    block_b = text_lines[:, ROWS_A:]
    image_lines = jnp.concatenate([image_pooled.T, image_proj], axis=1)

    ahead_b, back_b = [shift(block_b, "z", 1)], [shift(block_b, "z", -1)]
    block_a = join([block_a] + [shift(block_a, "x", step) for step in (1, -1, 2)])
    block_a, ahead_b[0], back_b[0], image_lines = together(block_a, ahead_b[0], back_b[0], image_lines)

    low = jnp.concatenate([block_b, ahead_b[0], back_b[0]], axis=0)
    ahead_low = shift(low, "x", 1)
    ahead_a, back_a = [shift(block_a, "z", 1)], [shift(block_a, "z", -1)]
    ahead_b.append(shift(ahead_b[0], "z", 1))
    back_b.append(shift(back_b[0], "z", -1))
    spread = jnp.broadcast_to(image_lines[None], (SIZES["y"],) + image_lines.shape)
    image_own = lax.all_to_all(spread, "y", 0, 0).reshape(-1, image_lines.shape[1])
    ahead_a[0], back_a[0], ahead_b[1], back_b[1], ahead_low = together(
        ahead_a[0], back_a[0], ahead_b[1], back_b[1], ahead_low
    )

    ahead_a.append(shift(ahead_a[0], "z", 1))
    back_a.append(shift(back_a[0], "z", -1))
    ahead_b.append(shift(ahead_b[1], "z", 1))
    back_b.append(shift(back_b[1], "z", -1))
    far_b = shift(ahead_b[2], "z", 1)
    back_low = shift(low, "x", -1)
    high = [after(ahead_b[1], ahead_b[2]), after(back_b[1], ahead_b[2])]
    high += [after(ahead_b[2], far_b), after(back_b[2], far_b), far_b]
    high = jnp.concatenate(high, axis=0)
    ahead_a[1], back_a[1], high, back_low = together(ahead_a[1], back_a[1], high, back_low)

    ahead_a.append(shift(ahead_a[1], "z", 1))
    back_a.append(shift(back_a[1], "z", -1))
    ahead_high, back_high = shift(high, "x", 1), shift(high, "x", -1)
    ahead_a[2], back_a[2], ahead_high, back_high, image_own = together(
        ahead_a[2], back_a[2], ahead_high, back_high, image_own
    )

    far_a = shift(ahead_a[2], "z", 1)
    far_low, far_high = shift(ahead_low, "x", 1), shift(back_high, "x", -1)
    image_other = shift(image_own, "core", 1)
    image_unit = image_units(rows, image_own, image_other)

    text_a, weight_own = split_chunks(in_turn(block_a, ahead_a, back_a), depth)
    weight_other = shift(weight_own, "core", 1)
    far_other = shift(far_a, "core", 1)
    lows = [low, ahead_low, back_low, far_low]
    highs = [high, ahead_high, back_high, far_high]
    logits, col_part, row_part = score(
        depth,
        core.reshape(1),
        teacher_scale,
        weight_own,
        weight_other,
        far_a,
        far_other,
        image_unit,
        text_a,
        lows,
        highs,
    )
    col_part = col_part.reshape(columns // 128, 128)
    spread = jnp.broadcast_to(col_part[None], (32,) + col_part.shape)
    col_lse = add_exp(lax.all_to_all(spread, IMG, 0, 0)).reshape(-1)

    row_part = row_part.reshape(rows // 128, 128)
    row_part = add_exp(jnp.stack([row_part, shift(row_part, "core", 1)]))
    row_parts = [row_part] + [shift(row_part, "y", step) for step in (1, -1, 2)]
    row_lse = add_exp(jnp.stack(row_parts)).reshape(-1)
    image_targets = minus(logits, row_lse[:, None])
    text_targets = minus(logits, col_lse[None, :])
    return (image_targets, text_targets)


def solution(mesh):
    grid = Mesh(mesh.devices.reshape(8, 4, 4, 2), ("z", "x", "y", "core"))
    placed = (P(IMG, TXT), P(TXT, IMG), P(TXT, None), P(IMG, None), P())
    return jax.shard_map(
        on_device,
        mesh=grid,
        in_specs=placed,
        out_specs=(P(IMG, TXT), P(IMG, TXT)),
        check_vma=False,
    )
```
